32 devices in a mesh: groups: 2 (over x), dp: 16 (over z, y, core).
Axes of the slice: x: 2, y: 2, z: 4, core: 2. Of those that a mesh axis runs over, the one named last changes fastest.
Arguments:
- images: bfloat16 [16, 128, 128, 320], P('groups', 'dp'), parts along dimension 0, may hold values from -6 to 6
- kernel_weights: bfloat16 [16, 2, 3, 3, 320, 320], P('dp'), may hold values from -0.109375 to 0.109375
- kernel_momentum: float32 [16, 2, 3, 3, 320, 320], P('dp'), may hold values from -0.12 to 0.12
- kernel_grads: bfloat16 [16, 2, 3, 3, 320, 320], P('dp'), may hold values from -0.119628906 to 0.119628906
- owners: int32 [2], replicated, may hold values from 0 to 15
Outputs:
- blocks_out: bfloat16 [16, 128, 128, 320], P('groups', 'dp'), parts along dimension 0
The draws below stay inside these ranges and needn't reach their ends.
There are 2 independent parts, one for each index of `groups`. The reference program is written for one: setup_inputs(seed, part) draws one part's arguments, and reference() takes and returns one part's arrays. A program takes and returns all parts, laid end to end along the dimension named above; an argument that names none is the same for every part. Nothing has to cross between parts.
Inputs may be any that keep to these rules, and one draw needn't show every extreme that they name: `owners`: each entry is a slot index along the first dimension of the kernel state.
All inputs are finite; a program needn't handle non-finite values.
Results may differ from the reference program's by a relative error of at most 0.0095.
Values may be sent and summed in bfloat16 or wider, within the bound.
No kernel may reach another device: no remote copies, remote signals or barrier semaphores. Data moves between devices by JAX's collectives and lax.ppermute only.
A program may use at most 128 MiB of HBM per device.

```python
import jax
import jax.numpy as jnp
from jax import lax

C = 320
IMGS = 8
WIDTH = 128
HEIGHT = 128
N_DP = 16


def level_of(own_key, dims, shards, low, high):
    level = 1.0
    for axis_at, blocks in shards:
        steps = jax.random.uniform(jax.random.fold_in(jax.random.fold_in(own_key, 6), axis_at), (blocks,), jnp.float32, low / len(shards), high / len(shards))
        level = level * jnp.repeat(jnp.exp(steps), dims[axis_at] // blocks).reshape((-1,) + (1,) * (len(dims) - 1 - axis_at))
    return level


def centred(own_key, dims, scale, most, shards=(), kind=jnp.bfloat16):
    gain = level_of(own_key, dims, shards, -0.22, 0.18) if shards else 1.0
    result = jax.random.normal(own_key, dims, jnp.float32) * scale * gain
    return jnp.minimum(jnp.maximum(result, -most), most).astype(kind)


def setup_inputs(seed: int = 0, part: int = 0) -> dict:
    keys = jax.random.split(jax.random.key(seed), 6)
    part_splits = jax.random.split(jax.random.fold_in(keys[5], part), 6)
    return {
        "images": centred(part_splits[0], (IMGS, HEIGHT, WIDTH, C), 1.0, 6.0, ((1, 16),)),
        "kernel_weights": centred(keys[1], (N_DP, 2, 3, 3, C, C), (9 * C) ** -0.5, 0.109375, ((0, 16),)),
        "kernel_momentum": centred(keys[2], (N_DP, 2, 3, 3, C, C), 0.02, 0.12, ((0, 16),), jnp.float32),
        "kernel_grads": centred(keys[3], (N_DP, 2, 3, 3, C, C), 0.02, 0.119628906, ((0, 16),)),
        "owners": jax.random.randint(keys[4], (2,), 0, N_DP).astype(jnp.int32),
    }


momentum_decay = 0.9
learn_rate = 0.5


def convolve(activated, kernel):
    return lax.conv_general_dilated(activated, kernel, (1, 1), ((1, 1), (1, 1)), dimension_numbers=("NHWC", "HWIO", "NHWC"), preferred_element_type=jnp.float32)


def reference(images, kernel_weights, kernel_momentum, kernel_grads, owners):
    kernels = []
    for kernel_index in range(2):
        slot = owners[kernel_index]
        velocity = momentum_decay * kernel_momentum[slot, kernel_index] + kernel_grads[slot, kernel_index].astype(jnp.float32)
        updated = kernel_weights[slot, kernel_index].astype(jnp.float32) - learn_rate * velocity
        kernels.append(updated.astype(jnp.bfloat16))
    activated = jax.nn.silu(images.astype(jnp.float32)).astype(jnp.bfloat16)
    hidden = (images.astype(jnp.float32) + convolve(activated, kernels[0])).astype(jnp.bfloat16)
    activated = jax.nn.silu(hidden.astype(jnp.float32)).astype(jnp.bfloat16)
    return (hidden.astype(jnp.float32) + convolve(activated, kernels[1])).astype(jnp.bfloat16)
```

```python
import functools

import jax
import jax.numpy as jnp
from jax import lax
from jax.experimental import pallas as pl
from jax.experimental.pallas import tpu as pltpu
from jax.sharding import PartitionSpec as P

momentum_decay = 0.9
learn_rate = 0.5
axes = ("groups", "dp")
lanes = 128


def silu(v):
    half = v.astype(jnp.float32) * 0.5
    return (half * jnp.tanh(half) + half).astype(jnp.bfloat16)


def update_body(place, w_ref, m_ref, g_ref, mine0, mine1, theirs0, theirs1, *, depth):
    core = place[2]
    step = pl.program_id(0)
    first = (2 * place[0] + lax.bitwise_xor(place[1], step)) * 2 * lanes
    for row in range(w_ref.shape[1]):
        velocity = momentum_decay * m_ref[0, row] + g_ref[0, row].astype(jnp.float32)
        fresh = w_ref[0, row].astype(jnp.float32) - learn_rate * velocity
        at = first + lax.broadcasted_iota(jnp.int32, fresh.shape, 0)
        fresh = jnp.where(at < depth, fresh, 0.0)
        flipped = fresh.T.astype(jnp.bfloat16)
        low, high = flipped[:, :lanes], flipped[:, lanes:]
        own = jnp.where(core == 0, low, high)
        other = jnp.where(core == 0, high, low)

        @pl.when(step == 0)
        def _():
            mine0[row] = own
            theirs0[row] = other

        @pl.when(step == 1)
        def _():
            mine1[row] = own
            theirs1[row] = other


def update(place, weights, momentum, grads, which):
    taps, depth, outs = weights.shape[1:]
    block = pl.BlockSpec(
        (1, taps, 2 * lanes, outs),
        lambda i, place: (which, 0, 2 * place[0] + lax.bitwise_xor(place[1], i), 0),
    )
    piece = pl.BlockSpec((taps, outs, lanes), lambda i, place: (0, 0, 0))
    return pl.pallas_call(
        functools.partial(update_body, depth=depth),
        grid_spec=pltpu.PrefetchScalarGridSpec(
            num_scalar_prefetch=1, grid=(2,), in_specs=[block] * 3, out_specs=[piece] * 4
        ),
        out_shape=[jax.ShapeDtypeStruct((taps, outs, lanes), jnp.bfloat16)] * 4,
        compiler_params=pltpu.CompilerParams(vmem_limit_bytes=40 * 2**20),
        name="kernel_update",
    )(place, weights, momentum, grads)


def swap(x, groups, count, change):
    pairs = []
    for g in range(groups):
        for d in range(count):
            to_g, to_d = change(g, d)
            pairs.append((g * count + d, to_g * count + to_d))
    return lax.ppermute(x, axes, pairs)


def spread(pieces, owner, groups, count):
    dp = lax.axis_index("dp")
    differs = lax.bitwise_xor(dp, owner)
    mine0, mine1, theirs0, theirs1 = pieces

    def swap_dp(x, bit):
        return swap(x, groups, count, lambda g, d: (g, d ^ bit))

    def keep(bit, own, got):
        return jnp.where(lax.bitwise_and(differs, bit) == 0, own, got)

    got1 = swap_dp(theirs1, 1)
    got0 = swap_dp(theirs0, 1)
    far = keep(1, mine1, got1)
    near = keep(1, mine0, got0)
    piece = keep(2, near, swap_dp(far, 2))
    bit = count // 2
    while bit >= 4:
        piece = keep(bit, piece, swap_dp(piece, bit))
        bit //= 2
    ring = [
        piece,
        swap_dp(piece, 2),
        swap(piece, groups, count, lambda g, d: (g ^ 1, d)),
        swap(piece, groups, count, lambda g, d: (g ^ 1, d ^ 2)),
    ]
    return ring + [swap_dp(x, 1) for x in ring]


def conv_body(place, x_ref, up_ref, down_ref, *rest):
    piece_refs, (out_ref, top_ref, bottom_ref, mixed, shifted) = rest[:8], rest[8:]
    n, rows, chans, cols = x_ref.shape
    depth = 3 * chans

    @pl.when(pl.program_id(0) == 0)
    def _():
        for relation, ref in enumerate(piece_refs):
            tile = (
                4 * lax.bitwise_xor(place[0], (relation >> 1) & 1)
                + 2 * lax.bitwise_xor(place[1], relation & 1)
                + lax.bitwise_xor(place[2], relation >> 2)
            )
            at = pl.ds(pl.multiple_of(tile * lanes, lanes), lanes)
            outer = (ref[0].astype(jnp.float32) + ref[2].astype(jnp.float32)) * 0.5
            inner = ref[1].astype(jnp.float32) * 0.5
            mixed[0, :, at] = ref[0]
            mixed[1, :, at] = (outer + inner).astype(jnp.bfloat16)
            mixed[2, :, at] = (outer - inner).astype(jnp.bfloat16)
            mixed[3, :, at] = ref[2]

    def put(row):
        for i in range(n):
            raw = up_ref[i] if row == 0 else down_ref[i] if row == rows + 1 else x_ref[i, row - 1]
            act = silu(raw)
            lane = lax.broadcasted_iota(jnp.int32, act.shape, 1)
            zero = jnp.zeros_like(act)
            at = pl.ds(i * cols, cols)
            shifted[row, 0:chans, at] = jnp.where(lane == 0, zero, pltpu.roll(act, 1, 1))
            shifted[row, chans : 2 * chans, at] = act
            shifted[row, 2 * chans : depth, at] = jnp.where(
                lane == cols - 1, zero, pltpu.roll(act, cols - 1, 1)
            )

    def product(t, field):
        return jnp.dot(mixed[t, :, 0:depth], field, preferred_element_type=jnp.float32)

    def emit(row, i, branch):
        result = (x_ref[i, row].astype(jnp.float32) + branch).astype(out_ref.dtype)
        out_ref[i, row] = result
        if row == 0:
            top_ref[i] = result
        if row == rows - 1:
            bottom_ref[i] = result

    for row in range(4):
        put(row)
    for block in range(rows // 2):
        if block + 1 < rows // 2:
            put(2 * block + 4)
            put(2 * block + 5)
        d = [shifted.at[2 * block + j] for j in range(4)]
        plus = product(1, d[1][...] + d[2][...])
        minus = product(2, d[2][...] - d[1][...])
        even = plus + minus + product(0, d[0][...] - d[2][...])
        odd = plus - minus - product(3, d[1][...] - d[3][...])
        for i in range(n):
            at = slice(i * cols, (i + 1) * cols)
            emit(2 * block, i, even[:, at])
            emit(2 * block + 1, i, odd[:, at])


def residual_conv(place, field, up, down, pieces):
    images, rows, chans, cols = field.shape
    n = 2
    strip = pl.BlockSpec((n, rows, chans, cols), lambda i, place: (i, 0, 0, 0))
    edge = pl.BlockSpec((n, chans, cols), lambda i, place: (i, 0, 0))
    piece = pl.BlockSpec(pieces[0].shape, lambda i, place: (0, 0, 0))
    return pl.pallas_call(
        conv_body,
        grid_spec=pltpu.PrefetchScalarGridSpec(
            num_scalar_prefetch=1,
            grid=(images // n,),
            in_specs=[strip, edge, edge] + [piece] * 8,
            out_specs=[strip, edge, edge],
            scratch_shapes=[
                pltpu.VMEM((4, chans, 8 * lanes), jnp.bfloat16),
                pltpu.VMEM((rows + 2, 3 * chans, n * cols), jnp.bfloat16),
            ],
        ),
        out_shape=[
            jax.ShapeDtypeStruct(field.shape, field.dtype),
            jax.ShapeDtypeStruct(up.shape, field.dtype),
            jax.ShapeDtypeStruct(up.shape, field.dtype),
        ],
        compiler_params=pltpu.CompilerParams(vmem_limit_bytes=40 * 2**20),
        cost_estimate=pl.CostEstimate(
            flops=2 * images * rows * cols * 9 * chans * chans,
            bytes_accessed=4 * images * rows * cols * chans,
            transcendentals=images * rows * cols * chans,
        ),
        name="residual_conv",
    )(place, field, up, down, *pieces)


def borders(top, bottom, count):
    up = lax.ppermute(bottom, "dp", [(i, i + 1) for i in range(count - 1)])
    down = lax.ppermute(top, "dp", [(i + 1, i) for i in range(count - 1)])
    return up, down


def local(groups, count, images, kernel_weights, kernel_momentum, kernel_grads, owners):
    g, dp = lax.axis_index("groups"), lax.axis_index("dp")
    place = jnp.stack([g % 2, (dp // 2) % 2, dp % 2]).astype(jnp.int32)

    def flat(x):
        _, kernels, taps, across, ins, outs = x.shape
        return x.reshape(kernels, taps, across * ins, outs)

    state = [flat(x) for x in (kernel_weights, kernel_momentum, kernel_grads)]
    first = spread(update(place, *state, 0), owners[0], groups, count)
    second = spread(update(place, *state, 1), owners[1], groups, count)
    field = jnp.swapaxes(images, 2, 3)
    up, down = borders(field[:, 0], field[:, -1], count)
    hidden, top, bottom = residual_conv(place, field, up, down, first)
    up, down = borders(top, bottom, count)
    result = residual_conv(place, hidden, up, down, second)[0]
    return jnp.swapaxes(result, 2, 3)


def solution(mesh):
    groups, count = mesh.shape["groups"], mesh.shape["dp"]
    assert groups % 2 == 0 and count % 4 == 0 and count & (count - 1) == 0
    state = P("dp", None, None, None, None, None)
    return jax.shard_map(
        functools.partial(local, groups, count),
        mesh=mesh,
        in_specs=(P("groups", "dp", None, None), state, state, state, P()),
        out_specs=P("groups", "dp", None, None),
        check_vma=False,
    )
```

```python
import functools

import jax
import jax.numpy as jnp
from jax import lax
from jax.experimental import pallas as pl
from jax.experimental.pallas import tpu as pltpu
from jax.sharding import PartitionSpec as P

momentum_decay = 0.9
learn_rate = 0.5
axes = ("groups", "dp")
lanes = 128


def silu(v):
    half = v.astype(jnp.float32) * 0.5
    return (half * jnp.tanh(half) + half).astype(jnp.bfloat16)


def bits_of(ids, split):
    g, dp = ids[0], ids[1]
    return lax.rem(g, 2), lax.bitwise_and(lax.div(dp, split), 1), lax.bitwise_and(dp, 1)


def tile_pair(ids, kernel, step, splits):
    split = jnp.where(kernel == 0, splits[0], splits[1])
    half, bit, _ = bits_of(ids, split)
    return 2 * half + lax.bitwise_xor(bit, step)


def update_body(ids, owners, w_ref, m_ref, g_ref, *refs, depth, splits):
    kernel, step = pl.program_id(0), pl.program_id(1)
    core = lax.bitwise_and(ids[1], 1)
    taps, _, outs = w_ref.shape[1:]
    first = tile_pair(ids, kernel, step, splits) * 2 * lanes

    @pl.when(owners[kernel] == ids[1])
    def _():
        for tap in range(taps):
            velocity = momentum_decay * m_ref[0, tap] + g_ref[0, tap].astype(jnp.float32)
            fresh = w_ref[0, tap].astype(jnp.float32) - learn_rate * velocity
            at = first + lax.broadcasted_iota(jnp.int32, fresh.shape, 0)
            flipped = jnp.where(at < depth, fresh, 0.0).astype(jnp.bfloat16).T
            low, high = flipped[:, :lanes], flipped[:, lanes:]
            own = jnp.where(core == 0, low, high)
            other = jnp.where(core == 0, high, low)
            for at_step in range(2):

                @pl.when(step == at_step)
                def _():
                    refs[at_step][kernel, tap] = own
                    refs[2 + at_step][kernel, tap] = other


def update(ids, owners, weights, momentum, grads, splits):
    kernels, taps, depth, outs = weights.shape

    def which(k, i, ids, owners):
        last = (owners[1] == ids[1]).astype(jnp.int32)
        mine = owners[k] == ids[1]
        k = jnp.where(mine, k, last)
        return (k, 0, tile_pair(ids, k, jnp.where(mine, i, k * (1 - last)), splits), 0)

    block = pl.BlockSpec((1, taps, 2 * lanes, outs), which)
    shape = (kernels, taps, outs, lanes)
    return pl.pallas_call(
        functools.partial(update_body, depth=depth, splits=splits),
        grid_spec=pltpu.PrefetchScalarGridSpec(
            num_scalar_prefetch=2,
            grid=(kernels, 2),
            in_specs=[block] * 3,
            out_specs=[pl.BlockSpec(shape, lambda k, i, ids, owners: (0, 0, 0, 0))] * 4,
        ),
        out_shape=[jax.ShapeDtypeStruct(shape, jnp.bfloat16)] * 4,
        compiler_params=pltpu.CompilerParams(vmem_limit_bytes=62 * 2**20),
        name="kernel_update",
    )(ids, owners, weights, momentum, grads)


def swap(x, groups, count, change):
    pairs = []
    for g in range(groups):
        for d in range(count):
            to_g, to_d = change(g, d)
            pairs.append((g * count + d, to_g * count + to_d))
    return lax.ppermute(x, axes, pairs)


def after(x, other, owners):
    return jnp.where(owners[0] < 0, other, x)


def spread(pieces, owners, splits, groups, count):
    differs = lax.bitwise_xor(lax.axis_index("dp"), owners)
    mine0, mine1, theirs0, theirs1 = pieces

    def swap_dp(x, bit):
        return swap(x, groups, count, lambda g, d: (g, d ^ bit))

    def keep(bit, own, got, kernel):
        return jnp.where(lax.bitwise_and(differs[kernel], bit) == 0, own, got)

    got1 = swap_dp(theirs1, 1)
    got0 = swap_dp(theirs0, 1)
    far = [keep(1, mine1[k], got1[k], k) for k in range(2)]
    near = [keep(1, mine0[k], got0[k], k) for k in range(2)]
    held = [keep(splits[k], near[k], swap_dp(far[k], splits[k]), k) for k in range(2)]
    high = [1 << b for b in range(3, count.bit_length() - 1)]
    turns = (high[::-1] + [2], [4] + high[::-1])
    for bits in zip(*turns):
        held[0] = after(held[0], held[1], owners)
        held = [keep(bits[k], held[k], swap_dp(held[k], bits[k]), k) for k in range(2)]
    return after(held[0], held[1], owners), held[1]


def gather(piece, split, groups, count):
    def move(x, bit, group):
        return swap(x, groups, count, lambda g, d: (g ^ group, d ^ bit))

    return [piece, move(piece, split, 0), move(piece, 0, 1), move(piece, split, 1)]


def gather_cores(ring, groups, count):
    return ring + [swap(x, groups, count, lambda g, d: (g, d ^ 1)) for x in ring]


def conv_body(ids, *refs, split, rows, blocks, sources, drains, waits):
    piece_refs, refs = refs[:8], refs[8:]
    source_refs, refs = refs[: len(sources)], refs[len(sources) + waits :]
    drain_refs, (mixed, shifted) = refs[: len(drains)], refs[len(drains) :]
    where_in = {row: (at, pos) for at, held in enumerate(sources) for pos, row in enumerate(held)}
    n, _, chans, cols = source_refs[0].shape
    depth = 3 * chans

    @pl.when(pl.program_id(0) == 0)
    def _():
        half, bit, core = bits_of(ids, split)
        for relation, ref in enumerate(piece_refs):
            tile = (
                4 * lax.bitwise_xor(half, (relation >> 1) & 1)
                + 2 * lax.bitwise_xor(bit, relation & 1)
                + lax.bitwise_xor(core, relation >> 2)
            )
            at = pl.ds(pl.multiple_of(tile * lanes, lanes), lanes)
            outer = (ref[0].astype(jnp.float32) + ref[2].astype(jnp.float32)) * 0.5
            inner = ref[1].astype(jnp.float32) * 0.5
            mixed[0, :, at] = ref[0]
            mixed[1, :, at] = (outer + inner).astype(jnp.bfloat16)
            mixed[2, :, at] = (outer - inner).astype(jnp.bfloat16)
            mixed[3, :, at] = ref[2]

    def load(row, i):
        at, pos = where_in[row]
        return source_refs[at][i, pos]

    done = set()

    def put(row):
        if row in done:
            return
        done.add(row)
        for i in range(n):
            act = silu(load(row, i))
            lane = lax.broadcasted_iota(jnp.int32, act.shape, 1)
            zero = jnp.zeros_like(act)
            at = pl.ds(i * cols, cols)
            shifted[row + 1, 0:chans, at] = jnp.where(lane == 0, zero, pltpu.roll(act, 1, 1))
            shifted[row + 1, chans : 2 * chans, at] = act
            shifted[row + 1, 2 * chans : depth, at] = jnp.where(
                lane == cols - 1, zero, pltpu.roll(act, cols - 1, 1)
            )

    def product(t, field):
        return jnp.dot(mixed[t, :, 0:depth], field, preferred_element_type=jnp.float32)

    def emit(row, i, branch):
        result = (load(row, i).astype(jnp.float32) + branch).astype(jnp.bfloat16)
        for ref, held in zip(drain_refs, drains):
            if row in held:
                ref[i, held.index(row)] = result

    for row in range(2 * blocks[0] - 1, 2 * blocks[0] + 3):
        put(row)
    for at, block in enumerate(blocks):
        if at + 1 < len(blocks):
            for row in range(2 * blocks[at + 1] - 1, 2 * blocks[at + 1] + 3):
                put(row)
        d = [shifted.at[2 * block + j] for j in range(4)]
        plus = product(1, d[1][...] + d[2][...])
        minus = product(2, d[2][...] - d[1][...])
        even = plus + minus + product(0, d[0][...] - d[2][...])
        odd = plus - minus - product(3, d[1][...] - d[3][...])
        for i in range(n):
            at = slice(i * cols, (i + 1) * cols)
            emit(2 * block, i, even[:, at])
            emit(2 * block + 1, i, odd[:, at])
    made = {row for block in blocks for row in (2 * block, 2 * block + 1)}
    for ref, held in zip(drain_refs, drains):
        for pos, row in enumerate(held):
            if row not in made:
                at = len(sources) - 1
                for i in range(n):
                    ref[i, pos] = source_refs[at][i, sources[at].index(("made", row))]


def residual_conv(ids, split, pieces, rows, blocks, sources, drains, waits=()):
    held, arrays = zip(*sources)
    images, _, chans, cols = arrays[0].shape
    n = 2

    def strip(count):
        return pl.BlockSpec((n, count, chans, cols), lambda i, ids: (i, 0, 0, 0))

    piece = pl.BlockSpec(pieces[0].shape, lambda i, ids: (0, 0, 0))
    return pl.pallas_call(
        functools.partial(
            conv_body, split=split, rows=rows, blocks=blocks, sources=held, drains=drains, waits=len(waits)
        ),
        grid_spec=pltpu.PrefetchScalarGridSpec(
            num_scalar_prefetch=1,
            grid=(images // n,),
            in_specs=[piece] * 8
            + [strip(len(x)) for x in held]
            + [pl.BlockSpec(memory_space=pl.ANY)] * len(waits),
            out_specs=[strip(len(x)) for x in drains],
            scratch_shapes=[
                pltpu.VMEM((4, chans, 8 * lanes), jnp.bfloat16),
                pltpu.VMEM((rows + 2, 3 * chans, n * cols), jnp.bfloat16),
            ],
        ),
        out_shape=[
            jax.ShapeDtypeStruct((images, len(x), chans, cols), jnp.bfloat16) for x in drains
        ],
        compiler_params=pltpu.CompilerParams(vmem_limit_bytes=28 * 2**20),
        cost_estimate=pl.CostEstimate(
            flops=4 * images * len(blocks) * cols * 9 * chans * chans,
            bytes_accessed=4 * images * rows * cols * chans,
            transcendentals=images * rows * cols * chans,
        ),
        name="residual_conv",
    )(ids, *pieces, *arrays, *waits)


def borders(top, bottom, count):
    up = lax.ppermute(bottom, "dp", [(i, i + 1) for i in range(count - 1)])
    down = lax.ppermute(top, "dp", [(i + 1, i) for i in range(count - 1)])
    return up, down


def local(groups, count, images, kernel_weights, kernel_momentum, kernel_grads, owners):
    g, dp = lax.axis_index("groups"), lax.axis_index("dp")
    splits = (4, 2)
    ids = jnp.stack([g, dp]).astype(jnp.int32)

    def flat(x):
        _, kernels, taps, across, ins, outs = x.shape
        return x.reshape(kernels, taps, across * ins, outs)

    state = [flat(x) for x in (kernel_weights, kernel_momentum, kernel_grads)]
    field = jnp.swapaxes(images, 2, 3)
    rows = field.shape[1]
    everything = tuple(range(rows))
    up, down = borders(field[:, :1], field[:, -1:], count)

    one, two = spread(update(ids, owners, *state, splits), owners, splits, groups, count)
    ring = gather(one, splits[0], groups, count)
    first = gather_cores(ring, groups, count)
    two = after(two, ring[3], owners)
    ring = gather(two, splits[1], groups, count)

    around = [((-1,), up), ((rows,), down)]
    hidden, top, bottom = residual_conv(
        ids,
        splits[0],
        first,
        rows,
        tuple(range(rows // 2)),
        [(everything, field)] + around,
        (everything, (0,), (rows - 1,)),
        (two,),
    )
    ring = [after(x, top[: x.shape[0], 0], owners) for x in ring]
    second = gather_cores(ring, groups, count)
    up, down = borders(top, bottom, count)
    edge_blocks, inner_blocks = (0, rows // 2 - 1), tuple(range(1, rows // 2 - 1))
    inner = everything[2:-2]
    around = [((-1,), up), ((rows,), down)]
    parts = [(everything, hidden)]
    (out_inner,) = residual_conv(ids, splits[1], second, rows, inner_blocks, parts, (inner,))
    made = [(tuple(("made", row) for row in inner), out_inner)]
    (out,) = residual_conv(ids, splits[1], second, rows, edge_blocks, parts + around + made, (everything,))
    return jnp.swapaxes(out, 2, 3)


def solution(mesh):
    groups, count = mesh.shape["groups"], mesh.shape["dp"]
    assert groups % 2 == 0 and count % 8 == 0 and count & (count - 1) == 0
    state = P("dp", None, None, None, None, None)
    return jax.shard_map(
        functools.partial(local, groups, count),
        mesh=mesh,
        in_specs=(P("groups", "dp", None, None), state, state, state, P()),
        out_specs=P("groups", "dp", None, None),
        check_vma=False,
    )
```

```python
import functools

import jax
import jax.numpy as jnp
from jax import lax
from jax.experimental import pallas as pl
from jax.experimental.pallas import tpu as pltpu
from jax.sharding import PartitionSpec as P

momentum_decay = 0.9
learn_rate = 0.5
axes = ("groups", "dp")
lanes = 128
group = 4


def silu(v):
    half = v.astype(jnp.float32) * 0.5
    return (half * jnp.tanh(half) + half).astype(jnp.bfloat16)


def bits_of(ids, split):
    g, dp = ids[0], ids[1]
    return lax.rem(g, 2), lax.bitwise_and(lax.div(dp, split), 1), lax.bitwise_and(dp, 1)


def tile_pair(ids, kernel, step, splits):
    split = jnp.where(kernel == 0, splits[0], splits[1])
    half, bit, _ = bits_of(ids, split)
    return 2 * half + lax.bitwise_xor(bit, step)


def update_body(ids, owners, w_ref, m_ref, g_ref, *refs, depth, splits):
    kernel, step = pl.program_id(0), pl.program_id(1)
    core = lax.bitwise_and(ids[1], 1)
    taps, _, outs = w_ref.shape[1:]
    first = tile_pair(ids, kernel, step, splits) * 2 * lanes

    @pl.when(owners[kernel] == ids[1])
    def _():
        for tap in range(taps):
            velocity = momentum_decay * m_ref[0, tap] + g_ref[0, tap].astype(jnp.float32)
            fresh = w_ref[0, tap].astype(jnp.float32) - learn_rate * velocity
            at = first + lax.broadcasted_iota(jnp.int32, fresh.shape, 0)
            flipped = jnp.where(at < depth, fresh, 0.0).astype(jnp.bfloat16).T
            low, high = flipped[:, :lanes], flipped[:, lanes:]
            own = jnp.where(core == 0, low, high)
            other = jnp.where(core == 0, high, low)
            for at_step in range(2):

                @pl.when(step == at_step)
                def _():
                    refs[at_step][kernel, tap] = own
                    refs[2 + at_step][kernel, tap] = other


def update(ids, owners, weights, momentum, grads, splits):
    kernels, taps, depth, outs = weights.shape

    def which(k, i, ids, owners):
        last = (owners[1] == ids[1]).astype(jnp.int32)
        mine = owners[k] == ids[1]
        k = jnp.where(mine, k, last)
        return (k, 0, tile_pair(ids, k, jnp.where(mine, i, k * (1 - last)), splits), 0)

    block = pl.BlockSpec((1, taps, 2 * lanes, outs), which)
    shape = (kernels, taps, outs, lanes)
    return pl.pallas_call(
        functools.partial(update_body, depth=depth, splits=splits),
        grid_spec=pltpu.PrefetchScalarGridSpec(
            num_scalar_prefetch=2,
            grid=(kernels, 2),
            in_specs=[block] * 3,
            out_specs=[pl.BlockSpec(shape, lambda k, i, ids, owners: (0, 0, 0, 0))] * 4,
        ),
        out_shape=[jax.ShapeDtypeStruct(shape, jnp.bfloat16)] * 4,
        compiler_params=pltpu.CompilerParams(vmem_limit_bytes=57 * 2**20),
        name="kernel_update",
    )(ids, owners, weights, momentum, grads)


def swap(x, groups, count, change):
    pairs = []
    for g in range(groups):
        for d in range(count):
            to_g, to_d = change(g, d)
            pairs.append((g * count + d, to_g * count + to_d))
    return lax.ppermute(x, axes, pairs)


def after(x, other, owners):
    return jnp.where(owners[0] < 0, other, x)


def spread(pieces, owners, splits, groups, count, edges_after):
    differs = lax.bitwise_xor(lax.axis_index("dp"), owners)
    mine0, mine1, theirs0, theirs1 = pieces

    def swap_dp(x, bit):
        return swap(x, groups, count, lambda g, d: (g, d ^ bit))

    def keep(bit, own, got, kernel):
        return jnp.where(lax.bitwise_and(differs[kernel], bit) == 0, own, got)

    got1 = swap_dp(theirs1, 1)
    got0 = swap_dp(theirs0, 1)
    far = [keep(1, mine1[k], got1[k], k) for k in range(2)]
    near = [keep(1, mine0[k], got0[k], k) for k in range(2)]
    held = [keep(splits[k], near[k], swap_dp(far[k], splits[k]), k) for k in range(2)]
    edge_rows = edges_after(far[0])
    held[0] = after(held[0], edge_rows[1][: held[0].shape[0], 0], owners)
    high = [1 << b for b in range(3, count.bit_length() - 1)]
    turns = (high[::-1] + [4], [2] + high[::-1])
    for bits in zip(*turns):
        held[0] = after(held[0], held[1], owners)
        held = [keep(bits[k], held[k], swap_dp(held[k], bits[k]), k) for k in range(2)]
    return edge_rows, (after(held[0], held[1], owners), held[1])


def gather(piece, split, groups, count):
    def move(x, bit, group):
        return swap(x, groups, count, lambda g, d: (g ^ group, d ^ bit))

    return [piece, move(piece, split, 0), move(piece, 0, 1), move(piece, split, 1)]


def gather_cores(ring, groups, count):
    return ring + [swap(x, groups, count, lambda g, d: (g, d ^ 1)) for x in ring]


def mix(ids, split, piece_refs, mixed):
    half, bit, core = bits_of(ids, split)
    for relation, ref in enumerate(piece_refs):
        tile = (
            4 * lax.bitwise_xor(half, (relation >> 1) & 1)
            + 2 * lax.bitwise_xor(bit, relation & 1)
            + lax.bitwise_xor(core, relation >> 2)
        )
        at = pl.ds(pl.multiple_of(tile * lanes, lanes), lanes)
        outer = (ref[0].astype(jnp.float32) + ref[2].astype(jnp.float32)) * 0.5
        inner = ref[1].astype(jnp.float32) * 0.5
        mixed[0, :, at] = ref[0]
        mixed[1, :, at] = (outer + inner).astype(jnp.bfloat16)
        mixed[2, :, at] = (outer - inner).astype(jnp.bfloat16)
        mixed[3, :, at] = ref[2]


def put(shifted, slot, raws):
    for i, raw in enumerate(raws):
        shifted[slot, :, pl.ds(i * raw.shape[1], raw.shape[1])] = silu(raw)


def three_columns(field, cols):
    chans, width = field.shape
    lane = lax.broadcasted_iota(jnp.int32, (chans, cols), 1)
    zero = jnp.zeros((chans, cols), field.dtype)
    parts = [field[:, at : at + cols] for at in range(0, width, cols)]
    left = [jnp.where(lane == 0, zero, pltpu.roll(x, 1, 1)) for x in parts]
    right = [jnp.where(lane == cols - 1, zero, pltpu.roll(x, cols - 1, 1)) for x in parts]
    return jnp.concatenate(
        [jnp.concatenate(left, axis=1), field, jnp.concatenate(right, axis=1)], axis=0
    )


def two_rows(mixed, shifted, slot, cols=lanes):
    d = [shifted[slot + j] for j in range(4)]
    depth, step = 3 * shifted.shape[1], 2 * lanes

    def product(t, field):
        wide = three_columns(field, cols)
        parts = [slice(at, min(at + step, depth)) for at in range(0, depth, step)]
        return sum(
            jnp.dot(mixed[t, :, at], wide[at], preferred_element_type=jnp.float32) for at in parts
        )

    plus = product(1, d[1] + d[2])
    minus = product(2, d[2] - d[1])
    even = plus + minus + product(0, d[0] - d[2])
    odd = plus - minus - product(3, d[1] - d[3])
    return even, odd


def add(raw, branch, i):
    cols = raw.shape[1]
    return (raw.astype(jnp.float32) + branch[:, i * cols : (i + 1) * cols]).astype(jnp.bfloat16)


def whole_body(ids, *refs, split, count):
    *arrays, mixed, shifted = refs[8:11] + refs[-5:]
    pl.when(pl.program_id(0) == 0)(lambda: mix(ids, split, refs[:8], mixed))
    for pair in range(arrays[0].shape[0] // 2):
        parts = [x.at[2 * pair : 2 * pair + 2] for x in arrays]
        whole_pair(ids, *parts, mixed, shifted.at[pair], count=count)


def whole_pair(ids, x, core, outer, out, core_out, outer_out, mixed, shifted, *, count):
    n, rows = x.shape[:2]
    dp = ids[1]
    first_core = lax.bitwise_and(dp, 1) == 0

    def raw(row, i):
        if 0 <= row < rows:
            return x[i, row]
        ends = (outer[i, 0], core[i, 0]) if row < 0 else (core[i, 0], outer[i, 0])
        edge = jnp.where(first_core, *ends)
        inside = dp > 0 if row < 0 else dp < count - 1
        return jnp.where(inside, edge, jnp.zeros_like(edge))

    for row in range(-1, 3):
        put(shifted, row + 1, [raw(row, i) for i in range(n)])
    for block in range(rows // 2):
        if block + 1 < rows // 2:
            for row in (2 * block + 3, 2 * block + 4):
                put(shifted, row + 1, [raw(row, i) for i in range(n)])
        made = two_rows(mixed, shifted, 2 * block)
        for row, branch in zip((2 * block, 2 * block + 1), made):
            for i in range(n):
                result = add(x[i, row], branch, i)
                out[i, row] = result
                if row in (0, rows - 1):
                    facing = core_out, outer_out
                    for ref, faces in zip(facing, (~first_core, first_core)):

                        @pl.when(faces if row == 0 else ~faces)
                        def _():
                            ref[i, 0] = result


def near_body(ids, *refs, split, count):
    *arrays, mixed, shifted = refs[8:]
    pl.when(pl.program_id(0) == 0)(lambda: mix(ids, split, refs[:8], mixed))
    for pair in range(arrays[0].shape[0] // 2):
        parts = [x.at[2 * pair : 2 * pair + 2] for x in arrays]
        near_pair(ids, *parts, mixed, shifted.at[pair])


def near_pair(ids, x, core, out, mixed, shifted):
    n, rows = x.shape[:2]
    first_core = lax.bitwise_and(ids[1], 1) == 0
    last = rows // 2 - 1
    for row in range(5):
        put(shifted, row + 1, [x[i, row] for i in range(n)])
    for block in range(1, last + 1):
        at = block
        for row in range(2 * block + 3, min(2 * block + 5, rows)):
            put(shifted, row + 1, [x[i, row] for i in range(n)])
        if block == last - 1:
            put(shifted, jnp.where(first_core, rows + 1, 0), [core[i, 0] for i in range(n)])
        if block == last:
            at = jnp.where(first_core, last, 0)
        for step, branch in enumerate(two_rows(mixed, shifted, 2 * at)):
            for i in range(n):
                out[i, 2 * at + step] = add(x[i, 2 * at + step], branch, i)


def far_body(ids, *refs, split, count):
    x, outer, _, out, mixed, shifted = refs[8:]
    pl.when(pl.program_id(0) == 0)(lambda: mix(ids, split, refs[:8], mixed))
    for pair in range(x.shape[0] // 2):
        parts = [x.at[2 * pair : 2 * pair + 2] for x in (x, outer, out)]
        far_pair(ids, *parts, mixed, shifted.at[pair], count=count)


def far_pair(ids, x, outer, out, mixed, shifted, *, count):
    n, rows = x.shape[:2]
    dp = ids[1]
    first_core = lax.bitwise_and(dp, 1) == 0
    inside = jnp.where(first_core, dp > 0, dp < count - 1)
    near = jnp.where(first_core, 0, rows - 2)
    edge = [jnp.where(inside, outer[i, 0], jnp.zeros_like(outer[i, 0])) for i in range(n)]
    put(shifted, 0, [jnp.where(first_core, edge[i], x[i, rows - 3]) for i in range(n)])
    put(shifted, 1, [x[i, near] for i in range(n)])
    put(shifted, 2, [x[i, near + 1] for i in range(n)])
    put(shifted, 3, [jnp.where(first_core, x[i, 2], edge[i]) for i in range(n)])
    for step, branch in enumerate(two_rows(mixed, shifted, 0)):
        for i in range(n):
            out[i, step] = add(x[i, near + step], branch, i)


def conv_call(body, ids, split, count, pieces, operands, specs, outs, out_specs, share, limit, **more):
    images, rows, chans, cols = operands[0].shape
    return pl.pallas_call(
        functools.partial(body, split=split, count=count),
        grid_spec=pltpu.PrefetchScalarGridSpec(
            num_scalar_prefetch=1,
            grid=(images // group,),
            in_specs=[pl.BlockSpec(pieces[0].shape, lambda i, ids: (0, 0, 0))] * 8 + specs,
            out_specs=out_specs,
            scratch_shapes=[
                pltpu.VMEM((4, chans, 8 * lanes), jnp.bfloat16),
                pltpu.VMEM((group // 2, rows + 2, chans, 2 * cols), jnp.bfloat16),
            ],
        ),
        out_shape=[jax.ShapeDtypeStruct((images, x, chans, cols), jnp.bfloat16) for x in outs],
        compiler_params=pltpu.CompilerParams(vmem_limit_bytes=limit * 2**20),
        cost_estimate=pl.CostEstimate(
            flops=share * 2 * images * rows * cols * 9 * chans * chans // 4,
            bytes_accessed=4 * images * rows * cols * chans,
            transcendentals=images * rows * cols * chans,
        ),
        name="residual_conv",
        **more,
    )(ids, *pieces, *operands)


def strip(field, height, block=None):
    shape = (group, height) + field.shape[2:]
    if block is None:
        return pl.BlockSpec(shape, lambda i, ids: (i, 0, 0, 0))
    return pl.BlockSpec(shape, lambda i, ids: (i, lax.bitwise_and(ids[1], 1) * block, 0, 0))


def edges_body(ids, x, _, held, core_out, outer_out):
    rows = x.shape[1]
    first_core = lax.bitwise_and(ids[1], 1) == 0
    held[...] = x[...]
    core_out[:, 0] = x[:, jnp.where(first_core, rows - 1, 0)]
    outer_out[:, 0] = x[:, jnp.where(first_core, 0, rows - 1)]


def edges(ids, field, wait):
    images, rows, chans, cols = field.shape
    whole, edge = strip(field, rows), strip(field, 1)
    return pl.pallas_call(
        edges_body,
        grid_spec=pltpu.PrefetchScalarGridSpec(
            num_scalar_prefetch=1,
            grid=(images // group,),
            in_specs=[whole, pl.BlockSpec(memory_space=pl.ANY)],
            out_specs=[whole, edge, edge],
        ),
        out_shape=[
            jax.ShapeDtypeStruct((images, x, chans, cols), field.dtype) for x in (rows, 1, 1)
        ],
        compiler_params=pltpu.CompilerParams(vmem_limit_bytes=28 * 2**20),
        cost_estimate=pl.CostEstimate(
            flops=0, bytes_accessed=4 * images * rows * cols * chans, transcendentals=0
        ),
        name="edge_rows",
    )(ids, field, wait)


def borders(core, outer, groups, count):
    def across(g, d):
        to = d + (1 if d % 2 else -1)
        return g, to if 0 <= to < count else d

    return swap(core, groups, count, lambda g, d: (g, d ^ 1)), swap(outer, groups, count, across)


def local(groups, count, images, kernel_weights, kernel_momentum, kernel_grads, owners):
    g, dp = lax.axis_index("groups"), lax.axis_index("dp")
    splits = (2, 4)
    ids = jnp.stack([g, dp]).astype(jnp.int32)

    def flat(x):
        _, kernels, taps, across, ins, outs = x.shape
        return x.reshape(kernels, taps, across * ins, outs)

    state = [flat(x) for x in (kernel_weights, kernel_momentum, kernel_grads)]
    field = jnp.swapaxes(images, 2, 3)
    rows = field.shape[1]
    assert rows % 4 == 0 and rows >= 8
    fresh = update(ids, owners, *state, splits)
    (field, core, outer), (one, two) = spread(
        fresh, owners, splits, groups, count, functools.partial(edges, ids, field)
    )
    core, outer = borders(core, outer, groups, count)
    ring = gather(one, splits[0], groups, count)
    first = gather_cores(ring, groups, count)
    two = after(two, ring[3], owners)
    ring = gather(two, splits[1], groups, count)

    whole, edge, anywhere = strip(field, rows), strip(field, 1), pl.BlockSpec(memory_space=pl.ANY)
    hidden, core, outer = conv_call(
        whole_body,
        ids,
        splits[0],
        count,
        first,
        (field, core, outer, two),
        [whole, edge, edge, anywhere],
        (rows, 1, 1),
        [whole, edge, edge],
        4,
        28,
    )
    ring = [after(x, core[: x.shape[0], 0], owners) for x in ring]
    second = gather_cores(ring, groups, count)
    core, outer = borders(core, outer, groups, count)
    (out,) = conv_call(
        near_body,
        ids,
        splits[1],
        count,
        second,
        (hidden, core),
        [whole, edge],
        (rows,),
        [whole],
        3,
        28,
    )
    (out,) = conv_call(
        far_body,
        ids,
        splits[1],
        count,
        second,
        (hidden, outer, out),
        [strip(field, rows // 2, 1), edge, anywhere],
        (rows,),
        [strip(field, 2, rows // 2 - 1)],
        1,
        28,
        input_output_aliases={11: 0},
    )
    return jnp.swapaxes(out, 2, 3)


def solution(mesh):
    groups, count = mesh.shape["groups"], mesh.shape["dp"]
    assert groups % 2 == 0 and count % 8 == 0 and count & (count - 1) == 0
    state = P("dp", None, None, None, None, None)
    return jax.shard_map(
        functools.partial(local, groups, count),
        mesh=mesh,
        in_specs=(P("groups", "dp", None, None), state, state, state, P()),
        out_specs=P("groups", "dp", None, None),
        check_vma=False,
    )
```

```python
import functools

import jax
import jax.numpy as jnp
from jax import lax
from jax.experimental import pallas as pl
from jax.experimental.pallas import tpu as pltpu
from jax.sharding import PartitionSpec as P

momentum_decay = 0.9
learn_rate = 0.5
axes = ("groups", "dp")
lanes = 128
group = 4


def silu(v):
    half = v.astype(jnp.float32) * 0.5
    return (half * jnp.tanh(half) + half).astype(jnp.bfloat16)


def bits_of(ids, split):
    g, dp = ids[0], ids[1]
    return lax.rem(g, 2), lax.bitwise_and(lax.div(dp, split), 1), lax.bitwise_and(dp, 1)


def tile_pair(ids, kernel, step, splits):
    split = jnp.where(kernel == 0, splits[0], splits[1])
    half, bit, _ = bits_of(ids, split)
    return 2 * half + lax.bitwise_xor(bit, step)


def update_body(ids, owners, w_ref, m_ref, g_ref, *refs, depth, splits):
    kernel, step = pl.program_id(0), pl.program_id(1)
    core = lax.bitwise_and(ids[1], 1)
    taps, _, outs = w_ref.shape[1:]
    first = tile_pair(ids, kernel, step, splits) * 2 * lanes

    @pl.when(owners[kernel] == ids[1])
    def _():
        for tap in range(taps):
            velocity = momentum_decay * m_ref[0, tap] + g_ref[0, tap].astype(jnp.float32)
            fresh = w_ref[0, tap].astype(jnp.float32) - learn_rate * velocity
            at = first + lax.broadcasted_iota(jnp.int32, fresh.shape, 0)
            flipped = jnp.where(at < depth, fresh, 0.0).astype(jnp.bfloat16).T
            low, high = flipped[:, :lanes], flipped[:, lanes:]
            own = jnp.where(core == 0, low, high)
            other = jnp.where(core == 0, high, low)
            for at_step in range(2):

                @pl.when(step == at_step)
                def _():
                    refs[at_step][kernel, tap] = own
                    refs[2 + at_step][kernel, tap] = other


def update(ids, owners, weights, momentum, grads, splits):
    kernels, taps, depth, outs = weights.shape

    def which(k, i, ids, owners):
        last = (owners[1] == ids[1]).astype(jnp.int32)
        mine = owners[k] == ids[1]
        k = jnp.where(mine, k, last)
        return (k, 0, tile_pair(ids, k, jnp.where(mine, i, k * (1 - last)), splits), 0)

    block = pl.BlockSpec((1, taps, 2 * lanes, outs), which)
    shape = (kernels, taps, outs, lanes)
    return pl.pallas_call(
        functools.partial(update_body, depth=depth, splits=splits),
        grid_spec=pltpu.PrefetchScalarGridSpec(
            num_scalar_prefetch=2,
            grid=(kernels, 2),
            in_specs=[block] * 3,
            out_specs=[pl.BlockSpec(shape, lambda k, i, ids, owners: (0, 0, 0, 0))] * 4,
        ),
        out_shape=[jax.ShapeDtypeStruct(shape, jnp.bfloat16)] * 4,
        compiler_params=pltpu.CompilerParams(vmem_limit_bytes=50 * 2**20),
        name="kernel_update",
    )(ids, owners, weights, momentum, grads)


def swap(x, groups, count, change):
    pairs = []
    for g in range(groups):
        for d in range(count):
            to_g, to_d = change(g, d)
            pairs.append((g * count + d, to_g * count + to_d))
    return lax.ppermute(x, axes, pairs)


def after(x, other, owners):
    return jnp.where(owners[0] < 0, other, x)


def spread(pieces, owners, splits, groups, count, edges_after):
    differs = lax.bitwise_xor(lax.axis_index("dp"), owners)
    mine0, mine1, theirs0, theirs1 = pieces

    def swap_dp(x, bit):
        return swap(x, groups, count, lambda g, d: (g, d ^ bit))

    def keep(bit, own, got, kernel):
        return jnp.where(lax.bitwise_and(differs[kernel], bit) == 0, own, got)

    got1 = swap_dp(theirs1, 1)
    got0 = swap_dp(theirs0, 1)
    far = [keep(1, mine1[k], got1[k], k) for k in range(2)]
    near = [keep(1, mine0[k], got0[k], k) for k in range(2)]
    held = [keep(splits[k], near[k], swap_dp(far[k], splits[k]), k) for k in range(2)]
    edge_rows = edges_after(far[0])
    held[0] = after(held[0], edge_rows[1][: held[0].shape[0], 0], owners)
    high = [1 << b for b in range(3, count.bit_length() - 1)]
    turns = (high[::-1] + [2], [4] + high[::-1])
    for bits in zip(*turns):
        held[0] = after(held[0], held[1], owners)
        held = [keep(bits[k], held[k], swap_dp(held[k], bits[k]), k) for k in range(2)]
    return edge_rows, (after(held[0], held[1], owners), held[1])


def gather(piece, split, groups, count):
    def move(x, bit, group):
        return swap(x, groups, count, lambda g, d: (g ^ group, d ^ bit))

    return [piece, move(piece, split, 0), move(piece, 0, 1), move(piece, split, 1)]


def gather_cores(ring, groups, count):
    return ring + [swap(x, groups, count, lambda g, d: (g, d ^ 1)) for x in ring]


def mix(ids, split, piece_refs, mixed):
    half, bit, core = bits_of(ids, split)
    for relation, ref in enumerate(piece_refs):
        tile = (
            4 * lax.bitwise_xor(half, (relation >> 1) & 1)
            + 2 * lax.bitwise_xor(bit, relation & 1)
            + lax.bitwise_xor(core, relation >> 2)
        )
        at = pl.ds(pl.multiple_of(tile * lanes, lanes), lanes)
        outer = (ref[0].astype(jnp.float32) + ref[2].astype(jnp.float32)) * 0.5
        inner = ref[1].astype(jnp.float32) * 0.5
        mixed[0, :, at] = ref[0]
        mixed[1, :, at] = (outer + inner).astype(jnp.bfloat16)
        mixed[2, :, at] = (outer - inner).astype(jnp.bfloat16)
        mixed[3, :, at] = ref[2]


def put(shifted, slot, raws):
    for i, raw in enumerate(raws):
        shifted[slot, :, pl.ds(i * raw.shape[1], raw.shape[1])] = silu(raw)


def three_columns(field, cols):
    chans, width = field.shape
    lane = lax.broadcasted_iota(jnp.int32, (chans, cols), 1)
    zero = jnp.zeros((chans, cols), field.dtype)
    parts = [field[:, at : at + cols] for at in range(0, width, cols)]
    left = [jnp.where(lane == 0, zero, pltpu.roll(x, 1, 1)) for x in parts]
    right = [jnp.where(lane == cols - 1, zero, pltpu.roll(x, cols - 1, 1)) for x in parts]
    return jnp.concatenate(
        [jnp.concatenate(left, axis=1), field, jnp.concatenate(right, axis=1)], axis=0
    )


def two_rows(mixed, shifted, slot, cols=lanes):
    d = [shifted[slot + j] for j in range(4)]
    depth, step = 3 * shifted.shape[1], 2 * lanes

    def product(t, field):
        wide = three_columns(field, cols)
        parts = [slice(at, min(at + step, depth)) for at in range(0, depth, step)]
        return sum(
            jnp.dot(mixed[t, :, at], wide[at], preferred_element_type=jnp.float32) for at in parts
        )

    plus = product(1, d[1] + d[2])
    minus = product(2, d[2] - d[1])
    even = plus + minus + product(0, d[0] - d[2])
    odd = plus - minus - product(3, d[1] - d[3])
    return even, odd


def add(raw, branch, i):
    cols = raw.shape[1]
    return (raw.astype(jnp.float32) + branch[:, i * cols : (i + 1) * cols]).astype(jnp.bfloat16)


def whole_body(ids, *refs, split, count):
    *arrays, mixed, shifted = refs[8:11] + refs[-5:]
    pl.when(pl.program_id(0) == 0)(lambda: mix(ids, split, refs[:8], mixed))
    for pair in range(arrays[0].shape[0] // 2):
        parts = [x.at[2 * pair : 2 * pair + 2] for x in arrays]
        whole_pair(ids, *parts, mixed, shifted.at[pair], count=count)


def whole_pair(ids, x, core, outer, out, core_out, outer_out, mixed, shifted, *, count):
    n, rows = x.shape[:2]
    dp = ids[1]
    first_core = lax.bitwise_and(dp, 1) == 0

    def raw(row, i):
        if 0 <= row < rows:
            return x[i, row]
        ends = (outer[i, 0], core[i, 0]) if row < 0 else (core[i, 0], outer[i, 0])
        edge = jnp.where(first_core, *ends)
        inside = dp > 0 if row < 0 else dp < count - 1
        return jnp.where(inside, edge, jnp.zeros_like(edge))

    for row in range(-1, 3):
        put(shifted, row + 1, [raw(row, i) for i in range(n)])
    for block in range(rows // 2):
        if block + 1 < rows // 2:
            for row in (2 * block + 3, 2 * block + 4):
                put(shifted, row + 1, [raw(row, i) for i in range(n)])
        made = two_rows(mixed, shifted, 2 * block)
        for row, branch in zip((2 * block, 2 * block + 1), made):
            for i in range(n):
                result = add(x[i, row], branch, i)
                out[i, row] = result
                if row in (0, rows - 1):
                    facing = core_out, outer_out
                    for ref, faces in zip(facing, (~first_core, first_core)):

                        @pl.when(faces if row == 0 else ~faces)
                        def _():
                            ref[i, 0] = result


def near_body(ids, *refs, split, count):
    *arrays, mixed, shifted = refs[8:]
    pl.when(pl.program_id(0) == 0)(lambda: mix(ids, split, refs[:8], mixed))
    for pair in range(arrays[0].shape[0] // 2):
        parts = [x.at[2 * pair : 2 * pair + 2] for x in arrays]
        near_pair(ids, *parts, mixed, shifted.at[pair])


def near_pair(ids, x, core, out, mixed, shifted):
    n, rows = x.shape[:2]
    first_core = lax.bitwise_and(ids[1], 1) == 0
    last = rows // 2 - 1
    for row in range(5):
        put(shifted, row + 1, [x[i, row] for i in range(n)])
    for block in range(1, last + 1):
        at = block
        for row in range(2 * block + 3, min(2 * block + 5, rows)):
            put(shifted, row + 1, [x[i, row] for i in range(n)])
        if block == last - 1:
            put(shifted, jnp.where(first_core, rows + 1, 0), [core[i, 0] for i in range(n)])
        if block == last:
            at = jnp.where(first_core, last, 0)
        for step, branch in enumerate(two_rows(mixed, shifted, 2 * at)):
            for i in range(n):
                out[i, 2 * at + step] = add(x[i, 2 * at + step], branch, i)


def far_body(ids, *refs, split, count):
    x, outer, _, out, mixed, shifted = refs[8:]
    pl.when(pl.program_id(0) == 0)(lambda: mix(ids, split, refs[:8], mixed))
    for pair in range(x.shape[0] // 2):
        parts = [x.at[2 * pair : 2 * pair + 2] for x in (x, outer, out)]
        far_pair(ids, *parts, mixed, shifted.at[pair], count=count)


def far_pair(ids, x, outer, out, mixed, shifted, *, count):
    n, rows = x.shape[:2]
    dp = ids[1]
    first_core = lax.bitwise_and(dp, 1) == 0
    inside = jnp.where(first_core, dp > 0, dp < count - 1)
    near = jnp.where(first_core, 0, rows - 2)
    edge = [jnp.where(inside, outer[i, 0], jnp.zeros_like(outer[i, 0])) for i in range(n)]
    put(shifted, 0, [jnp.where(first_core, edge[i], x[i, rows - 3]) for i in range(n)])
    put(shifted, 1, [x[i, near] for i in range(n)])
    put(shifted, 2, [x[i, near + 1] for i in range(n)])
    put(shifted, 3, [jnp.where(first_core, x[i, 2], edge[i]) for i in range(n)])
    for step, branch in enumerate(two_rows(mixed, shifted, 0)):
        for i in range(n):
            out[i, step] = add(x[i, near + step], branch, i)


def conv_call(body, ids, split, count, pieces, operands, specs, outs, out_specs, share, limit, **more):
    images, rows, chans, cols = operands[0].shape
    return pl.pallas_call(
        functools.partial(body, split=split, count=count),
        grid_spec=pltpu.PrefetchScalarGridSpec(
            num_scalar_prefetch=1,
            grid=(images // group,),
            in_specs=[pl.BlockSpec(pieces[0].shape, lambda i, ids: (0, 0, 0))] * 8 + specs,
            out_specs=out_specs,
            scratch_shapes=[
                pltpu.VMEM((4, chans, 8 * lanes), jnp.bfloat16),
                pltpu.VMEM((group // 2, rows + 2, chans, 2 * cols), jnp.bfloat16),
            ],
        ),
        out_shape=[jax.ShapeDtypeStruct((images, x, chans, cols), jnp.bfloat16) for x in outs],
        compiler_params=pltpu.CompilerParams(vmem_limit_bytes=limit * 2**20),
        cost_estimate=pl.CostEstimate(
            flops=share * 2 * images * rows * cols * 9 * chans * chans // 4,
            bytes_accessed=4 * images * rows * cols * chans,
            transcendentals=images * rows * cols * chans,
        ),
        name="residual_conv",
        **more,
    )(ids, *pieces, *operands)


def strip(field, height, block=None):
    shape = (group, height) + field.shape[2:]
    if block is None:
        return pl.BlockSpec(shape, lambda i, ids: (i, 0, 0, 0))
    return pl.BlockSpec(shape, lambda i, ids: (i, lax.bitwise_and(ids[1], 1) * block, 0, 0))


def edges_body(ids, x, _, held, core_out, outer_out):
    rows = x.shape[1]
    first_core = lax.bitwise_and(ids[1], 1) == 0
    held[...] = x[...]
    core_out[:, 0] = x[:, jnp.where(first_core, rows - 1, 0)]
    outer_out[:, 0] = x[:, jnp.where(first_core, 0, rows - 1)]


def edges(ids, field, wait):
    images, rows, chans, cols = field.shape
    whole, edge = strip(field, rows), strip(field, 1)
    return pl.pallas_call(
        edges_body,
        grid_spec=pltpu.PrefetchScalarGridSpec(
            num_scalar_prefetch=1,
            grid=(images // group,),
            in_specs=[whole, pl.BlockSpec(memory_space=pl.ANY)],
            out_specs=[whole, edge, edge],
        ),
        out_shape=[
            jax.ShapeDtypeStruct((images, x, chans, cols), field.dtype) for x in (rows, 1, 1)
        ],
        compiler_params=pltpu.CompilerParams(vmem_limit_bytes=28 * 2**20),
        cost_estimate=pl.CostEstimate(
            flops=0, bytes_accessed=4 * images * rows * cols * chans, transcendentals=0
        ),
        name="edge_rows",
    )(ids, field, wait)


def borders(core, outer, groups, count):
    def across(g, d):
        to = d + (1 if d % 2 else -1)
        return g, to if 0 <= to < count else d

    return swap(core, groups, count, lambda g, d: (g, d ^ 1)), swap(outer, groups, count, across)


def local(groups, count, images, kernel_weights, kernel_momentum, kernel_grads, owners):
    g, dp = lax.axis_index("groups"), lax.axis_index("dp")
    splits = (4, 2)
    ids = jnp.stack([g, dp]).astype(jnp.int32)

    def flat(x):
        _, kernels, taps, across, ins, outs = x.shape
        return x.reshape(kernels, taps, across * ins, outs)

    state = [flat(x) for x in (kernel_weights, kernel_momentum, kernel_grads)]
    field = jnp.swapaxes(images, 2, 3)
    rows = field.shape[1]
    assert rows % 4 == 0 and rows >= 8
    fresh = update(ids, owners, *state, splits)
    (field, core, outer), (one, two) = spread(
        fresh, owners, splits, groups, count, functools.partial(edges, ids, field)
    )
    core, outer = borders(core, outer, groups, count)
    ring = gather(one, splits[0], groups, count)
    first = gather_cores(ring, groups, count)
    two = after(two, ring[3], owners)
    ring = gather(two, splits[1], groups, count)

    whole, edge, anywhere = strip(field, rows), strip(field, 1), pl.BlockSpec(memory_space=pl.ANY)
    hidden, core, outer = conv_call(
        whole_body,
        ids,
        splits[0],
        count,
        first,
        (field, core, outer, two),
        [whole, edge, edge, anywhere],
        (rows, 1, 1),
        [whole, edge, edge],
        4,
        28,
    )
    ring = [after(x, core[: x.shape[0], 0], owners) for x in ring]
    second = gather_cores(ring, groups, count)
    core, outer = borders(core, outer, groups, count)
    (out,) = conv_call(
        near_body,
        ids,
        splits[1],
        count,
        second,
        (hidden, core),
        [whole, edge],
        (rows,),
        [whole],
        3,
        28,
    )
    (out,) = conv_call(
        far_body,
        ids,
        splits[1],
        count,
        second,
        (hidden, outer, out),
        [strip(field, rows // 2, 1), edge, anywhere],
        (rows,),
        [strip(field, 2, rows // 2 - 1)],
        1,
        28,
        input_output_aliases={11: 0},
    )
    return jnp.swapaxes(out, 2, 3)


def solution(mesh):
    groups, count = mesh.shape["groups"], mesh.shape["dp"]
    assert groups % 2 == 0 and count % 8 == 0 and count & (count - 1) == 0
    state = P("dp", None, None, None, None, None)
    return jax.shard_map(
        functools.partial(local, groups, count),
        mesh=mesh,
        in_specs=(P("groups", "dp", None, None), state, state, state, P()),
        out_specs=P("groups", "dp", None, None),
        check_vma=False,
    )
```
